256 devices in a mesh: expert: 64 (over z, y, x_hi), dp: 4 (over x_lo, core).
Axes of the slice: x: 4 (x_hi: 2, x_lo: 2; x = x_hi * 2 + x_lo), y: 4, z: 8, core: 2. Of those that a mesh axis runs over, the one named last changes fastest.
Arguments:
- tokens: bfloat16 [3072, 7168], P(('expert', 'dp')), may hold values from -6 to 6
- expert_ids: int32 [3072, 8], P(('expert', 'dp')), may hold values from 0 to 63, all different within a row; in each aligned block of 12 rows (0 to 11, 12 to 23, ...) at most 2 rows name the same one
- gates: bfloat16 [3072, 8], P(('expert', 'dp')), may hold values from 0.049804688 to 1
- w_gate: bfloat16 [64, 7168, 1024], P('expert', None, 'dp'), may hold values from -0.0625 to 0.0625
- w_up: bfloat16 [64, 7168, 1024], P('expert', None, 'dp'), may hold values from -0.0625 to 0.0625
- w_down: bfloat16 [64, 1024, 7168], P('expert', 'dp'), may hold values from -0.1875 to 0.1875
Outputs:
- mixed_out: bfloat16 [3072, 7168], P(('expert', 'dp'))
The draws below stay inside these ranges and needn't reach their ends.
Inputs may be any that keep to these rules, and one draw needn't show every extreme that they name: `expert_ids`: each row names 8 different experts. Within the rows of one device (aligned blocks of 12 rows) no expert is named by more than 2 rows, a bound that some block reaches of some device in every draw.
All inputs are finite; a program needn't handle non-finite values.
Results may differ from the reference program's by a relative error of at most 0.015.
Values may be sent and summed in bfloat16 or wider, within the bound.
A program may use at most 128 MiB of HBM per device.

```python
import math
import jax
import jax.numpy as jnp
import numpy as np
from jax import lax

D = 7168
HIDDEN_SIZE = 1024
EXPERTS = 64
TOPK = 8
TOK_DEV = 12
CAP = 2
TOKENS = 3072
N_DP = 4


def steps_of(stream_key, shape, shards, smallest, high):
    def one(axis_at, shards_of):
        heights = jax.random.uniform(jax.random.fold_in(jax.random.fold_in(stream_key, 6), axis_at), (shards_of,), jnp.float32, smallest / len(shards), high / len(shards))
        return jnp.repeat(jnp.exp(heights), shape[axis_at] // shards_of).reshape((-1,) + (1,) * (len(shape) - axis_at - 1))

    level = one(*shards[0])
    for cut in shards[1:]:
        level = level * one(*cut)
    return level


def routed_block(key, own, number, rows, amount, top, limit, skew):
    order = jax.random.permutation(key, amount)
    packed, usual = load_shares(amount, rows * top, limit, skew, True), load_shares(amount, rows * top, limit, skew, False)
    places = jnp.arange(amount)

    def named(tallies, turn):
        used = int((tallies > 0).sum())
        fixed = max(1, used // 4)
        shifted = fixed + (places - fixed + turn * (used - fixed)) % max(1, amount - fixed)
        return jnp.zeros((amount,), jnp.int32).at[order[jnp.where(places < fixed, places, shifted)]].set(jnp.asarray(tallies, jnp.int32))

    tallies = jnp.where(number % 4 == 0, named(packed, number // 4), named(usual, number - number // 4 - 1))
    mixed = jax.random.permutation(jax.random.fold_in(own, 3), amount)
    giver, taker = mixed[0:amount // 2 * 2:2], mixed[1:amount // 2 * 2:2]
    room = jnp.minimum(tallies[giver] - 1, limit - tallies[taker]) // 2
    room = jnp.where((giver == order[0]) | (taker == order[0]) | (tallies[taker] == 0), 0, jnp.maximum(room, 0))
    shifted = jax.random.randint(jax.random.fold_in(own, 4), (amount // 2,), 0, 1 << 20) % (room + 1)
    tallies = tallies.at[giver].add(-shifted).at[taker].add(shifted)
    members = jnp.searchsorted(jnp.cumsum(tallies), jnp.arange(rows * top), side="right").astype(jnp.int32)
    table = members.reshape(top, rows).T
    table = table[jax.random.permutation(jax.random.fold_in(own, 1), rows)]
    turn = jax.random.randint(jax.random.fold_in(own, 2), (rows, 1), 0, top)
    return jnp.take_along_axis(table, (jnp.arange(top)[None, :] + turn) % top, axis=1)


def load_shares(number_of, total, limit, skew, full):
    weights = [(1 << 20) // math.isqrt(standing ** skew) + 1 for standing in range(1, number_of + 1)]
    largest = limit if full else min(limit, max(-(-total // number_of), total * weights[0] // sum(weights)))
    least = 1 if total - largest >= number_of - 1 else 0
    holding, surplus = [largest] + [least] * (number_of - 1), total - largest - least * (number_of - 1)
    while surplus > 0:
        candidates = [i for i in range(1, number_of) if holding[i] < largest] or [i for i in range(1, number_of) if holding[i] < limit]
        whole, remaining = sum([weights[i] for i in candidates]), surplus
        for i in candidates:
            extra = min(limit - holding[i], max(1, remaining * weights[i] // whole), surplus)
            holding[i] = holding[i] + extra
            surplus = surplus - extra
    return np.array(holding)


def noise(rng, dims, scale, bound, cuts=(), kind=jnp.bfloat16):
    entries = scale * jax.random.normal(rng, dims, jnp.float32)
    if cuts:
        entries = entries * steps_of(rng, dims, cuts, -0.22, 0.18)
    return jnp.clip(entries, -bound, bound).astype(kind)


def setup_inputs(seed: int = 0) -> dict:
    arg_keys = jax.random.split(jax.random.key(seed), 7)
    tokens = noise(arg_keys[0], (TOKENS, D), 1.0, 6.0, ((0, 256),))
    expert_ids_keys = jax.random.split(jax.random.fold_in(arg_keys[1], 1), TOKENS // TOK_DEV)
    expert_ids_turns = jax.random.permutation(jax.random.fold_in(arg_keys[1], 3), TOKENS // TOK_DEV)
    expert_ids = jax.vmap(lambda own, number: routed_block(jax.random.fold_in(arg_keys[1], 2), own, number, TOK_DEV, EXPERTS, TOPK, CAP, 2))(expert_ids_keys, expert_ids_turns).reshape((TOKENS, TOPK))
    gates = jnp.clip(jnp.exp(math.log(1.0) - 2.9996462 * jax.random.uniform(arg_keys[2], (TOKENS, TOPK), jnp.float32) ** steps_of(arg_keys[2], (TOKENS, TOPK), ((0, 256),), -0.2, 0.2)), 0.049804688, 1.0).astype(jnp.bfloat16)
    w_gate = noise(arg_keys[3], (EXPERTS, D, HIDDEN_SIZE), D ** -0.5, 0.0625, ((0, 64), (2, 4)))
    w_up = noise(arg_keys[4], (EXPERTS, D, HIDDEN_SIZE), D ** -0.5, 0.0625, ((0, 64), (2, 4)))
    w_down = noise(arg_keys[5], (EXPERTS, HIDDEN_SIZE, D), HIDDEN_SIZE ** -0.5, 0.1875, ((0, 64), (1, 4)))
    return dict(tokens=tokens, expert_ids=expert_ids, gates=gates, w_gate=w_gate, w_up=w_up, w_down=w_down)


def reference(tokens, expert_ids, gates, w_gate, w_up, w_down):
    block_count = TOKENS // TOK_DEV
    route_ids = expert_ids.reshape(block_count, TOK_DEV * TOPK).astype(jnp.int32)
    onehot = (route_ids[:, :, None] == jnp.arange(EXPERTS, dtype=jnp.int32)[None, None, :]).astype(jnp.int32)
    before = jnp.cumsum(onehot, axis=1).astype(jnp.int32) - onehot
    slot_index = jnp.sum(before * onehot, axis=2).astype(jnp.int32)
    block_index = jnp.broadcast_to(jnp.arange(block_count, dtype=jnp.int32)[:, None], route_ids.shape)
    token_index = (jnp.arange(TOKENS * TOPK, dtype=jnp.int32) // TOPK).reshape(route_ids.shape)
    row_table = jnp.full((EXPERTS, block_count, CAP), TOKENS, jnp.int32)
    row_table = row_table.at[route_ids, block_index, slot_index].set(token_index)
    weights_table = jnp.zeros((EXPERTS, block_count, CAP), jnp.float32)
    weights_table = weights_table.at[route_ids, block_index, slot_index].set(gates.reshape(route_ids.shape).astype(jnp.float32))
    padded = jnp.concatenate([tokens, jnp.zeros((1, D), tokens.dtype)], axis=0)
    block_width = HIDDEN_SIZE // N_DP

    def one_expert(expert_index, running):
        row_list = row_table[expert_index].reshape(-1)
        row_block = padded[row_list]
        gate_out = jnp.dot(row_block, w_gate[expert_index], preferred_element_type=jnp.float32)
        up_out = jnp.dot(row_block, w_up[expert_index], preferred_element_type=jnp.float32)
        hidden = (jax.nn.silu(gate_out) * up_out).astype(jnp.bfloat16)
        summed = jnp.zeros((row_list.shape[0], D), jnp.float32)
        for block_number in range(N_DP):
            low = block_number * block_width
            partial_out = jnp.dot(hidden[:, low:low + block_width], w_down[expert_index, low:low + block_width], preferred_element_type=jnp.float32)
            summed = summed + lax.optimization_barrier(partial_out.astype(jnp.bfloat16)).astype(jnp.float32)
        contribution = weights_table[expert_index].reshape(-1)[:, None] * summed
        return running.at[row_list].add(contribution)

    running = lax.fori_loop(0, EXPERTS, one_expert, jnp.zeros((TOKENS + 1, D), jnp.float32))
    return running[:TOKENS].astype(jnp.bfloat16)
```

```python
import functools

import jax
import jax.numpy as jnp
from jax import lax
from jax.experimental import pallas as pl
from jax.experimental.pallas import tpu as pltpu
from jax.sharding import PartitionSpec as P

CAP = 2
PAD = 16
YS = 4
CHUNK = 1024
MESH = pl.DeviceIdType.MESH


def dot(a, b):
    return jnp.dot(a, b, preferred_element_type=jnp.float32)


def kernel(
    zs, ys, n, width,
    tok_ref, ids_ref, gates_ref, wg_hbm, wu_hbm, wd_hbm, out_ref,
    ids16, gates16, mtsend, mtbuf, sel, zbuf, slot, rows, wg, wu, wd, acc_g, acc_u, hid,
    send_c, recv_c, send_x, recv_x, ret, retr, zsend, zrecv,
    w_sem, mt_sem, z_s, z_r, p_s, p_r, c_s, c_r, o_s, o_r, k_s, k_r,
    rc_s, rc_r, rx_s, rx_r, rp_s, rp_r, rz_s, rz_r,
):
    e = lax.axis_index("expert")
    q = lax.axis_index("dp")
    js = 2 * ys
    z, j = e // js, e % js
    y, xh = j // 2, j % 2
    xl, core = q // 2, q % 2
    tok_rows, topk = ids_ref.shape
    lanes = js * zs * CAP

    planes = []
    for dy in range(ys):
        for dx in range(2):
            if dy or dx:
                there = ((y + dy) % ys) * 2 + (xh + dx) % 2
                group = q if dx == 0 else (1 - xl) * 2 + core
                planes.append(((z * js + there, group), there, group))
    columns = []
    for dz in range(1, zs):
        there = (z + dz) % zs
        columns.append(((there * js + j, q), there))
    mate_q = xl * 2 + (1 - core)
    opp_q = (1 - xl) * 2 + core
    far_q = (1 - xl) * 2 + (1 - core)
    mate, opp = (e, mate_q), (e, opp_q)

    barrier = pltpu.get_barrier_semaphore()
    partners = [p[0] for p in planes] + [c[0] for c in columns] + [mate, opp]
    for partner in partners:
        pl.semaphore_signal(barrier, inc=1, device_id=partner, device_id_type=MESH)

    weights = [
        pltpu.make_async_copy(wg_hbm.at[0], wg, w_sem.at[0]),
        pltpu.make_async_copy(wu_hbm.at[0], wu, w_sem.at[1]),
    ] + [
        pltpu.make_async_copy(wd_hbm.at[0, :, pl.ds(c * width, width)], wd.at[c], w_sem.at[2 + c])
        for c in range(n)
    ]
    for copy in weights:
        copy.start()

    def remote(src, dst, send, recv, device):
        return pltpu.make_async_remote_copy(
            src_ref=src, dst_ref=dst, send_sem=send, recv_sem=recv,
            device_id=device, device_id_type=MESH,
        )

    ids16[...] = jnp.full(ids16.shape, -1, jnp.int32)
    ids16[0:tok_rows, :] = ids_ref[...]
    gates16[...] = jnp.zeros(gates16.shape, jnp.float32)
    gates16[0:tok_rows, :] = gates_ref[...].astype(jnp.float32)
    lane = lax.broadcasted_iota(jnp.int32, (PAD, lanes), 1)
    lane_expert = lane // (zs * CAP)
    lane_mine = (lane // CAP) % zs == z
    lane_slot = (lane % CAP).astype(jnp.float32)
    lower = (
        lax.broadcasted_iota(jnp.int32, (PAD, PAD), 0) > lax.broadcasted_iota(jnp.int32, (PAD, PAD), 1)
    ).astype(jnp.float32)
    for plane in range(zs):
        named = jnp.zeros((PAD, lanes), jnp.float32)
        weight = jnp.zeros((PAD, lanes), jnp.float32)
        for k in range(topk):
            match = ids16[:, k:k + 1] == lane_expert + plane * js
            named = named + jnp.where(match, 1.0, 0.0)
            weight = weight + jnp.where(match, gates16[:, k:k + 1], 0.0)
        before = dot(lower, named)
        mtsend[plane] = jnp.where((before == lane_slot) & lane_mine, weight, 0.0).astype(jnp.bfloat16)
    mtbuf[z] = mtsend[z]
    for c in range(n):
        zbuf[c, z] = jnp.zeros((PAD, width), jnp.bfloat16)
        zbuf[c, z, 0:tok_rows, :] = tok_ref[:, c * width:(c + 1) * width]

    pl.semaphore_wait(barrier, len(partners))

    for device, there in columns:
        remote(mtsend.at[there], mtbuf.at[z], mt_sem.at[0], mt_sem.at[1], device).start()

    def start_columns(c):
        for device, _ in columns:
            remote(zbuf.at[c, z], zbuf.at[c, z], z_s.at[c], z_r.at[c], device).start()

    for c in range(n):
        start_columns(c)

    acc_g[...] = jnp.zeros_like(acc_g)
    acc_u[...] = jnp.zeros_like(acc_u)
    all_mt = mtbuf.at[pl.ds(0, zs - 1)]
    all_mts = mtsend.at[pl.ds(0, zs - 1)]
    remote(all_mts, all_mt, mt_sem.at[0], mt_sem.at[1], mate).wait_recv()
    mixing = mtbuf[...].reshape(zs * PAD, lanes)
    sel[...] = jnp.where(mixing.astype(jnp.float32) != 0.0, 1.0, 0.0).T.astype(jnp.bfloat16)

    def wait_columns(buf, c, send, recv):
        part = buf.at[c, pl.ds(0, zs - 1)]
        return remote(part, part, send.at[c], recv.at[c], mate)

    def wait_planes(buf, c, send, recv):
        part = buf.at[c, pl.ds(0, js - 1)]
        return remote(part, part, send.at[c], recv.at[c], mate)

    def to_mate(c):
        return remote(rows.at[c, q], rows.at[c, q], c_s.at[c], c_r.at[c], mate)

    def to_opp(c):
        return remote(rows.at[c, q], rows.at[c, q], o_s.at[c], o_r.at[c], opp)

    def pass_on(c):
        return remote(rows.at[c, opp_q], rows.at[c, opp_q], k_s.at[c], k_r.at[c], mate)

    def dispatch(s, carry):
        @pl.when(s < n)
        def _():
            c = s
            wait_columns(zbuf, c, z_s, z_r).wait_recv()
            chosen = dot(sel[...], zbuf[c].reshape(zs * PAD, width)).astype(jnp.bfloat16)
            slot[c] = chosen.reshape(js, zs * CAP, width)
            for device, there, group in planes:
                remote(slot.at[c, there], rows.at[c, group, j], p_s.at[c], p_r.at[c], device).start()
            rows[c, q, j] = slot[c, j]

        @pl.when((s >= 1) & (s < n + 1))
        def _():
            c = s - 1
            wait_planes(slot, c, p_s, p_r).wait_recv()
            to_opp(c).start()
            to_mate(c).start()

        @pl.when((s >= 2) & (s < n + 2))
        def _():
            c = s - 2
            to_opp(c).wait_recv()
            pass_on(c).start()

        @pl.when(s == 3)
        def _():
            weights[0].wait()
            weights[1].wait()

        @pl.when(s >= 3)
        def _():
            c = s - 3
            to_mate(c).wait_recv()
            pass_on(c).wait_recv()
            block = rows[c].reshape(4 * lanes, width)
            depth = pl.ds(pl.multiple_of(c * width, width), width)
            acc_g[...] += dot(block, wg[depth, :])
            acc_u[...] += dot(block, wu[depth, :])

        return carry

    lax.fori_loop(0, n + 3, dispatch, 0)

    gate_out, up_out = acc_g[...], acc_u[...]
    hidden = gate_out / (1.0 + jnp.exp(-gate_out)) * up_out
    hid[...] = hidden.astype(jnp.bfloat16).reshape(hid.shape)
    for copy in weights[2:]:
        copy.wait()

    def sums_to_mate(c):
        return remote(send_c.at[c], recv_c.at[c], rc_s.at[c], rc_r.at[c], mate)

    def sums_to_opp(c):
        return remote(send_x.at[c], recv_x.at[c], rx_s.at[c], rx_r.at[c], opp)

    def combine(s, carry):
        @pl.when(s < n)
        def _():
            c = s
            for side in range(2):
                send_c[c, side] = dot(hid[side * 2 + (1 - core)], wd[c]).astype(jnp.bfloat16)
            sums_to_mate(c).start()

        @pl.when((s >= 1) & (s < n + 1))
        def _():
            c = s - 1
            sums_to_mate(c).wait_recv()
            total = dot(hid[opp_q], wd[c]) + recv_c[c, 1 - xl].astype(jnp.float32)
            send_x[c] = total.astype(jnp.bfloat16)
            sums_to_opp(c).start()

        @pl.when((s >= 2) & (s < n + 2))
        def _():
            c = s - 2
            sums_to_opp(c).wait_recv()
            total = (
                dot(hid[q], wd[c]) + recv_c[c, xl].astype(jnp.float32) + recv_x[c].astype(jnp.float32)
            )
            ret[c] = total.astype(jnp.bfloat16).reshape(js, zs * CAP, width)
            for device, there, _ in planes:
                remote(ret.at[c, there], retr.at[c, j], rp_s.at[c], rp_r.at[c], device).start()
            retr[c, j] = ret[c, j]

        @pl.when((s >= 3) & (s < n + 3))
        def _():
            c = s - 3
            wait_planes(retr, c, rp_s, rp_r).wait_recv()
            mixed = dot(mtbuf[...].reshape(zs * PAD, lanes), retr[c].reshape(lanes, width))
            zsend[c] = mixed.astype(jnp.bfloat16).reshape(zs, PAD, width)
            for device, there in columns:
                remote(zsend.at[c, there], zrecv.at[c, z], rz_s.at[c], rz_r.at[c], device).start()
            zrecv[c, z] = zsend[c, z]

        @pl.when(s >= 4)
        def _():
            c = s - 4
            wait_columns(zrecv, c, rz_s, rz_r).wait_recv()
            total = jnp.sum(zrecv[c].astype(jnp.float32), axis=0).astype(jnp.bfloat16)
            out_ref[:, pl.ds(pl.multiple_of(c * width, width), width)] = total[0:tok_rows]

        return carry

    lax.fori_loop(0, n + 4, combine, 0)

    remote(all_mts, all_mt, mt_sem.at[0], mt_sem.at[1], mate).wait_send()

    def finish(c, carry):
        wait_columns(zbuf, c, z_s, z_r).wait_send()
        wait_planes(slot, c, p_s, p_r).wait_send()
        to_mate(c).wait_send()
        to_opp(c).wait_send()
        pass_on(c).wait_send()
        sums_to_mate(c).wait_send()
        sums_to_opp(c).wait_send()
        wait_planes(ret, c, rp_s, rp_r).wait_send()
        wait_columns(zsend, c, rz_s, rz_r).wait_send()
        return carry

    lax.fori_loop(0, n, finish, 0)


def local(tokens, expert_ids, gates, w_gate, w_up, w_down):
    tok_rows, model_width = tokens.shape
    topk = expert_ids.shape[1]
    units = w_gate.shape[2]
    ys = YS
    js = 2 * ys
    zs = lax.axis_size("expert") // js
    width = min(CHUNK, model_width // 2)
    n = model_width // width
    lanes = js * zs * CAP
    held = zs * CAP
    bf = jnp.bfloat16
    vmem = pltpu.VMEM
    sems = lambda count: pltpu.SemaphoreType.DMA((count,))
    return pl.pallas_call(
        functools.partial(kernel, zs, ys, n, width),
        out_shape=jax.ShapeDtypeStruct((tok_rows, model_width), bf),
        in_specs=[pl.BlockSpec(memory_space=pltpu.VMEM)] * 3 + [pl.BlockSpec(memory_space=pl.ANY)] * 3,
        out_specs=pl.BlockSpec(memory_space=pltpu.VMEM),
        scratch_shapes=[
            vmem((PAD, topk), jnp.int32),
            vmem((PAD, topk), jnp.float32),
            vmem((zs, PAD, lanes), bf),
            vmem((zs, PAD, lanes), bf),
            vmem((lanes, zs * PAD), bf),
            vmem((n, zs, PAD, width), bf),
            vmem((n, js, held, width), bf),
            vmem((n, 4, js, held, width), bf),
            vmem((model_width, units), bf),
            vmem((model_width, units), bf),
            vmem((n, units, width), bf),
            vmem((4 * lanes, units), jnp.float32),
            vmem((4 * lanes, units), jnp.float32),
            vmem((4, lanes, units), bf),
            vmem((n, 2, lanes, width), bf),
            vmem((n, 2, lanes, width), bf),
            vmem((n, lanes, width), bf),
            vmem((n, lanes, width), bf),
            vmem((n, js, held, width), bf),
            vmem((n, js, held, width), bf),
            vmem((n, zs, PAD, width), bf),
            vmem((n, zs, PAD, width), bf),
            sems(2 + n),
            sems(2),
        ] + [sems(n)] * 18,
        compiler_params=pltpu.CompilerParams(
            collective_id=0, has_side_effects=True, vmem_limit_bytes=60 * 1024 * 1024
        ),
        cost_estimate=pl.CostEstimate(
            flops=2 * 4 * lanes * model_width * units * 3,
            bytes_accessed=3 * model_width * units * 2,
            transcendentals=4 * lanes * units,
        ),
    )(tokens, expert_ids, gates, w_gate, w_up, w_down)


def solution(mesh):
    in_specs = (
        P(("expert", "dp"), None),
        P(("expert", "dp"), None),
        P(("expert", "dp"), None),
        P("expert", None, "dp"),
        P("expert", None, "dp"),
        P("expert", "dp", None),
    )
    out_specs = P(("expert", "dp"), None)
    return jax.shard_map(local, mesh=mesh, in_specs=in_specs, out_specs=out_specs, check_vma=False)
```

```python
import functools

import jax
import jax.numpy as jnp
from jax import lax
from jax.experimental import pallas as pl
from jax.experimental.pallas import tpu as pltpu
from jax.sharding import PartitionSpec as P

CAP = 2
PAD = 16
YS = 4
CHUNK = 1024
KINDS = "aababab"
ORDER_OUT = (0, 1, 2, 3, 4, 5, 6)
ORDER_BACK = (6, 5, 4, 3, 2, 1, 0)
PACE_OUT = 1.2
PACE_BACK = 1.2
MESH = pl.DeviceIdType.MESH


def dot(a, b):
    return jnp.dot(a, b, preferred_element_type=jnp.float32)


def kernel(
    zs, ys, n, width,
    tok_ref, ids_ref, gates_ref, wg_hbm, wu_hbm, wd_hbm, out_ref,
    flip_i, flip_g, mtsend, mtbuf, mtopp, sel, zbuf, slot, rows, wg, wu, wd, acc_g, acc_u, hid,
    send_c, recv_c, send_x, recv_x, ret, retr, zsend, zrecv, last_s, last_r,
    w_sem, mt_sem, x_s, x_r, z_s, z_r, p_s, p_r, o_s, o_r, k_s, k_r,
    rc_s, rc_r, rx_s, rx_r, rp_s, rp_r, rz_s, rz_r, rl_s, rl_r,
):
    e = lax.axis_index("expert")
    q = lax.axis_index("dp")
    js = 2 * ys
    z, j = e // js, e % js
    y, xh = j // 2, j % 2
    xl, core = q // 2, q % 2
    topk, tok_rows = ids_ref.shape
    held = zs * CAP
    lanes = js * held
    kinds = [KINDS[c % len(KINDS)] for c in range(n)]

    planes = []
    for dy in range(ys):
        for dx in range(2):
            if dy or dx:
                there = ((y + dy) % ys) * 2 + (xh + dx) % 2
                side = xl if dx == 0 else 1 - xl
                planes.append(((z * js + there, side * 2 + core), there, side))
    columns = []
    for dz in range(1, zs):
        there = (z + dz) % zs
        columns.append(((there * js + j, q), there))
    long_hops, short_hops = zs // 2, zs - 1 - zs // 2
    step = 1 + core * (zs - 2)

    def at_z(hops, sign):
        return (z + zs * zs + sign * hops * step) % zs

    ahead, behind = (at_z(1, 1) * js + j, q), (at_z(1, -1) * js + j, q)
    mate = (e, xl * 2 + (1 - core))
    opp = (e, (1 - xl) * 2 + core)

    barrier = pltpu.get_barrier_semaphore()
    partners = [p[0] for p in planes] + [c[0] for c in columns] + [mate, opp]
    for partner in partners:
        pl.semaphore_signal(barrier, inc=1, device_id=partner, device_id_type=MESH)

    weights = [
        pltpu.make_async_copy(wg_hbm.at[0], wg, w_sem.at[0]),
        pltpu.make_async_copy(wu_hbm.at[0], wu, w_sem.at[1]),
    ] + [
        pltpu.make_async_copy(wd_hbm.at[0, :, pl.ds(c * width, width)], wd.at[c], w_sem.at[2 + c])
        for c in range(n)
    ]
    for copy in weights:
        copy.start()

    def remote(src, dst, send, recv, device):
        return pltpu.make_async_remote_copy(
            src_ref=src, dst_ref=dst, send_sem=send, recv_sem=recv,
            device_id=device, device_id_type=MESH,
        )

    for c in range(n):
        zbuf[c, z, 0] = jnp.zeros((PAD, width), jnp.bfloat16)
        zbuf[c, z, 0, 0:tok_rows, :] = tok_ref[:, c * width:(c + 1) * width]

    flip_i[...] = jnp.full(flip_i.shape, -1.0, jnp.float32)
    flip_i[0:topk, 0:tok_rows] = ids_ref[...].astype(jnp.float32)
    flip_g[...] = jnp.zeros(flip_g.shape, jnp.float32)
    flip_g[0:topk, 0:tok_rows] = gates_ref[...].astype(jnp.float32)
    ids = flip_i[...].T[0:PAD]
    gates = flip_g[...].T[0:PAD]
    lane = lax.broadcasted_iota(jnp.int32, (PAD, lanes), 1)
    lane_expert = lane // held
    lane_mine = (lane // CAP) % zs == z
    lane_slot = (lane % CAP).astype(jnp.float32)
    lower = (
        lax.broadcasted_iota(jnp.int32, (PAD, PAD), 0) > lax.broadcasted_iota(jnp.int32, (PAD, PAD), 1)
    ).astype(jnp.float32)
    for plane in range(zs):
        named = jnp.zeros((PAD, lanes), jnp.float32)
        weight = jnp.zeros((PAD, lanes), jnp.float32)
        for k in range(topk):
            match = ids[:, k:k + 1] == (lane_expert + plane * js).astype(jnp.float32)
            named = named + jnp.where(match, 1.0, 0.0)
            weight = weight + jnp.where(match, gates[:, k:k + 1], 0.0)
        before = dot(lower, named)
        mtsend[plane] = jnp.where((before == lane_slot) & lane_mine, weight, 0.0).astype(jnp.bfloat16)
    mtbuf[z] = mtsend[z]

    pl.semaphore_wait(barrier, len(partners))

    def sides(c):
        return 2 if kinds[c] == "b" else 1

    def swap_tokens(c):
        return remote(zbuf.at[c, z, 0], zbuf.at[c, z, 1], x_s.at[c], x_r.at[c], opp)

    def column_copy(c, origin, way, hop):
        part = zbuf.at[c, origin] if kinds[c] == "b" else zbuf.at[c, origin, 0]
        return remote(part, part, z_s.at[c], z_r.at[c, way * 4 + hop - 1], ahead if way == 0 else behind)

    def column_send(c, hop):
        if hop == 1:
            if kinds[c] == "b":
                swap_tokens(c).wait_recv()
            column_copy(c, z, 0, 1).start()
            column_copy(c, z, 1, 1).start()
            return
        if hop <= long_hops:
            column_copy(c, at_z(hop - 1, -1), 0, hop - 1).wait_recv()
            column_copy(c, at_z(hop - 1, -1), 0, hop).start()
        if hop <= short_hops:
            column_copy(c, at_z(hop - 1, 1), 1, hop - 1).wait_recv()
            column_copy(c, at_z(hop - 1, 1), 1, hop).start()

    def plane_send(c):
        column_copy(c, at_z(long_hops, -1), 0, long_hops).wait_recv()
        if short_hops:
            column_copy(c, at_z(short_hops, 1), 1, short_hops).wait_recv()
        for side in range(sides(c)):
            chosen = dot(sel[side], zbuf[c, :, side].reshape(zs * PAD, width)).astype(jnp.bfloat16)
            chosen = chosen.reshape(js, held, width)
            if kinds[c] == "a":
                slot[c, 0] = chosen
            else:
                for there in range(js):
                    slot[c, (xl + side + xh + there) % 2, there] = chosen[there]
        for device, there, dest in planes:
            for side in range(sides(c)):
                group = dest if kinds[c] == "a" else side
                src, dst = slot.at[c, side, there], rows.at[c, core, group, j]
                remote(src, dst, p_s.at[c], p_r.at[c], device).start()
        if kinds[c] == "a":
            rows[c, core, xl, j] = slot[c, 0, j]
        else:
            for side in range(2):
                rows[c, core, side, j] = slot[c, side, j]

    def plane_wait(buf, c, send, recv):
        part = buf.at[c, pl.ds(0, sides(c)), pl.ds(0, js - 1)]
        return remote(part, part, send.at[c], recv.at[c], mate)

    def to_opp(c):
        part = rows.at[c, core, xl]
        return remote(part, part, o_s.at[c], o_r.at[c], opp)

    def to_mate(c):
        part = rows.at[c, core]
        return remote(part, part, k_s.at[c], k_r.at[c], mate)

    def opp_send(c):
        plane_wait(slot, c, p_s, p_r).wait_recv()
        to_opp(c).start()

    def mate_send(c):
        if kinds[c] == "a":
            to_opp(c).wait_recv()
        else:
            plane_wait(slot, c, p_s, p_r).wait_recv()
        to_mate(c).start()

    multiplied = []

    def multiply(c):
        first = not multiplied
        multiplied.append(c)
        to_mate(c).wait_recv()
        if first:
            weights[0].wait()
            weights[1].wait()
        block = rows[c].reshape(4 * lanes, width)
        gate_part = dot(block, wg[c * width:(c + 1) * width, :])
        up_part = dot(block, wu[c * width:(c + 1) * width, :])
        acc_g[...] = gate_part if first else acc_g[...] + gate_part
        acc_u[...] = up_part if first else acc_u[...] + up_part

    def routes_out():
        for device, there in columns:
            remote(mtsend.at[there], mtbuf.at[z], mt_sem.at[0], mt_sem.at[1], device).start()

    def routes_wait():
        return remote(
            mtsend.at[pl.ds(0, zs - 1)], mtbuf.at[pl.ds(0, zs - 1)], mt_sem.at[0], mt_sem.at[1], mate
        )

    def routes_to_opp():
        return remote(mtbuf, mtopp, mt_sem.at[2], mt_sem.at[3], opp)

    def selection(buf):
        values = buf[...].reshape(zs * PAD, lanes).astype(jnp.float32)
        return jnp.where(values != 0.0, 1.0, 0.0).T.astype(jnp.bfloat16)

    def choose_own():
        routes_wait().wait_recv()
        routes_to_opp().start()
        sel[0] = selection(mtbuf)

    def choose_opp():
        routes_to_opp().wait_recv()
        sel[1] = selection(mtopp)

    both = [c for c in range(n) if kinds[c] == "b"]
    for c in both:
        swap_tokens(c).start()
    routes_out()
    tasks = []
    for place in range(n):
        c = [v for v in ORDER_OUT if v < n][place]
        at = place * PACE_OUT
        for hop in range(1, long_hops + 1):
            tasks.append((at + 1.6 * (hop - 1) - (2.0 if hop == 1 else 0.0), functools.partial(column_send, c, hop)))
        at += 1.6 * long_hops
        tasks.append((at, functools.partial(plane_send, c)))
        if kinds[c] == "a":
            tasks.append((at + 4.0, functools.partial(opp_send, c)))
            tasks.append((at + 11.0, functools.partial(mate_send, c)))
            at += 13.5
        else:
            tasks.append((at + 7.5, functools.partial(mate_send, c)))
            at += 10.0
        tasks.append((at, functools.partial(multiply, c)))
    tasks.append((1.5, choose_own))
    tasks.append((4.5, choose_opp))
    for _, task in sorted(tasks, key=lambda pair: pair[0]):
        task()

    gate_out, up_out = acc_g[...], acc_u[...]
    hidden = gate_out / (1.0 + jnp.exp(-gate_out)) * up_out
    hid[...] = hidden.astype(jnp.bfloat16).reshape(hid.shape)
    for copy in weights[2:]:
        copy.wait()

    def sums_to_mate(c):
        return remote(send_c.at[c], recv_c.at[c], rc_s.at[c], rc_r.at[c], mate)

    def sums_to_opp(c):
        return remote(send_x.at[c], recv_x.at[c], rx_s.at[c], rx_r.at[c], opp)

    def core_sums(c):
        block = hid[1 - core].reshape(2 * lanes, hid.shape[-1])
        send_c[c] = dot(block, wd[c]).astype(jnp.bfloat16).reshape(2, lanes, width)
        sums_to_mate(c).start()

    def chip_sums(c):
        sums_to_mate(c).wait_recv()
        total = dot(hid[core, 1 - xl], wd[c]) + recv_c[c, 1 - xl].astype(jnp.float32)
        send_x[c] = total.astype(jnp.bfloat16)
        sums_to_opp(c).start()

    def plane_return(c):
        if kinds[c] == "a":
            sums_to_opp(c).wait_recv()
            total = (
                dot(hid[core, xl], wd[c])
                + recv_c[c, xl].astype(jnp.float32)
                + recv_x[c].astype(jnp.float32)
            )
            ret[c, 0] = total.astype(jnp.bfloat16).reshape(js, held, width)
        else:
            sums_to_mate(c).wait_recv()
            for side in range(2):
                total = dot(hid[core, side], wd[c]) + recv_c[c, side].astype(jnp.float32)
                ret[c, side] = total.astype(jnp.bfloat16).reshape(js, held, width)
        for device, there, _ in planes:
            for side in range(sides(c)):
                src, dst = ret.at[c, side, there], retr.at[c, side, j]
                remote(src, dst, rp_s.at[c], rp_r.at[c], device).start()
        for side in range(sides(c)):
            retr[c, side, j] = ret[c, side, j]

    def return_copy(c, target, way, hop):
        src, dst = zsend.at[c, target], zrecv.at[c, way * 4 + hop - 1]
        if kinds[c] == "a":
            src, dst = src.at[0], dst.at[0]
        return remote(
            src, dst,
            rz_s.at[c], rz_r.at[c, way * 4 + hop - 1], ahead if way == 0 else behind,
        )

    def token_sums(c):
        plane_wait(retr, c, rp_s, rp_r).wait_recv()
        for side in range(sides(c)):
            if kinds[c] == "a":
                block = retr[c, 0].reshape(lanes, width)
            else:
                block = jnp.concatenate(
                    [retr[c, (xl + side + xh + there) % 2, there] for there in range(js)], axis=0
                )
            mixing = (mtbuf if side == 0 else mtopp)[...].reshape(zs * PAD, lanes)
            zsend[c, :, side] = dot(mixing, block).astype(jnp.bfloat16).reshape(zs, PAD, width)
        return_copy(c, at_z(long_hops, 1), 0, 1).start()

    def add_in(c, target, way, hop):
        for side in range(sides(c)):
            total = zsend[c, target, side].astype(jnp.float32)
            total = total + zrecv[c, way * 4 + hop - 1, side].astype(jnp.float32)
            zsend[c, target, side] = total.astype(jnp.bfloat16)

    def return_send(c, hop):
        target = at_z(long_hops - hop + 1, 1)
        return_copy(c, target, 0, hop - 1).wait_recv()
        add_in(c, target, 0, hop - 1)
        return_copy(c, target, 0, hop).start()
        hop = hop - (long_hops - short_hops)
        if hop >= 1:
            target = at_z(short_hops - hop + 1, -1)
            if hop >= 2:
                return_copy(c, target, 1, hop - 1).wait_recv()
                add_in(c, target, 1, hop - 1)
            return_copy(c, target, 1, hop).start()

    def column_total(c, side):
        total = zsend[c, z, side].astype(jnp.float32)
        total = total + zrecv[c, long_hops - 1, side].astype(jnp.float32)
        if short_hops:
            total = total + zrecv[c, 4 + short_hops - 1, side].astype(jnp.float32)
        return total

    def swap_sums(c):
        return remote(last_s.at[c], last_r.at[c], rl_s.at[c], rl_r.at[c], opp)

    def columns_done(c):
        return_copy(c, z, 0, long_hops).wait_recv()
        if short_hops:
            return_copy(c, z, 1, short_hops).wait_recv()
        if kinds[c] == "b":
            last_s[c] = column_total(c, 1).astype(jnp.bfloat16)
            swap_sums(c).start()
        else:
            out_ref[:, c * width:(c + 1) * width] = column_total(c, 0).astype(jnp.bfloat16)[0:tok_rows]

    def finish(c):
        swap_sums(c).wait_recv()
        total = column_total(c, 0) + last_r[c].astype(jnp.float32)
        out_ref[:, c * width:(c + 1) * width] = total.astype(jnp.bfloat16)[0:tok_rows]

    tasks = []
    for place in range(n):
        c = [v for v in ORDER_BACK if v < n][place]
        at = place * PACE_BACK
        tasks.append((at, functools.partial(core_sums, c)))
        if kinds[c] == "a":
            tasks.append((at + 2.5, functools.partial(chip_sums, c)))
            tasks.append((at + 9.5, functools.partial(plane_return, c)))
            at += 14.0
        else:
            tasks.append((at + 2.5, functools.partial(plane_return, c)))
            at += 10.0
        tasks.append((at, functools.partial(token_sums, c)))
        for hop in range(2, long_hops + 1):
            tasks.append((at + 1.6 * (hop - 1), functools.partial(return_send, c, hop)))
        at += 1.6 * long_hops
        tasks.append((at, functools.partial(columns_done, c)))
        if kinds[c] == "b":
            tasks.append((at + 2.0, functools.partial(finish, c)))
    for _, task in sorted(tasks, key=lambda pair: pair[0]):
        task()

    routes_wait().wait_send()
    routes_to_opp().wait_send()
    for c in range(n):
        if kinds[c] == "b":
            swap_tokens(c).wait_send()
            swap_sums(c).wait_send()
        else:
            to_opp(c).wait_send()
            sums_to_opp(c).wait_send()
        part = zbuf.at[c, pl.ds(0, zs - 1), pl.ds(0, sides(c))]
        remote(part, part, z_s.at[c], z_r.at[c, 0], mate).wait_send()
        plane_wait(slot, c, p_s, p_r).wait_send()
        to_mate(c).wait_send()
        sums_to_mate(c).wait_send()
        plane_wait(ret, c, rp_s, rp_r).wait_send()
        part = zsend.at[c, pl.ds(0, zs - 1), pl.ds(0, sides(c))]
        remote(part, part, rz_s.at[c], rz_r.at[c, 0], mate).wait_send()


def local(tokens, expert_ids, gates, w_gate, w_up, w_down):
    tok_rows, model_width = tokens.shape
    units = w_gate.shape[2]
    ys = YS
    js = 2 * ys
    zs = lax.axis_size("expert") // js
    width = min(CHUNK, model_width // 2)
    n = model_width // width
    held = zs * CAP
    lanes = js * held
    bf = jnp.bfloat16
    vmem = pltpu.VMEM
    sems = lambda *shape: pltpu.SemaphoreType.DMA(shape)
    return pl.pallas_call(
        functools.partial(kernel, zs, ys, n, width),
        out_shape=jax.ShapeDtypeStruct((tok_rows, model_width), bf),
        in_specs=[pl.BlockSpec(memory_space=pltpu.VMEM)] * 3 + [pl.BlockSpec(memory_space=pl.ANY)] * 3,
        out_specs=pl.BlockSpec(memory_space=pltpu.VMEM),
        scratch_shapes=[
            vmem((128, 128), jnp.float32),
            vmem((128, 128), jnp.float32),
            vmem((zs, PAD, lanes), bf),
            vmem((zs, PAD, lanes), bf),
            vmem((zs, PAD, lanes), bf),
            vmem((2, lanes, zs * PAD), bf),
            vmem((n, zs, 2, PAD, width), bf),
            vmem((n, 2, js, held, width), bf),
            vmem((n, 2, 2, js, held, width), bf),
            vmem((model_width, units), bf),
            vmem((model_width, units), bf),
            vmem((n, units, width), bf),
            vmem((4 * lanes, units), jnp.float32),
            vmem((4 * lanes, units), jnp.float32),
            vmem((2, 2, lanes, units), bf),
            vmem((n, 2, lanes, width), bf),
            vmem((n, 2, lanes, width), bf),
            vmem((n, lanes, width), bf),
            vmem((n, lanes, width), bf),
            vmem((n, 2, js, held, width), bf),
            vmem((n, 2, js, held, width), bf),
            vmem((n, zs, 2, PAD, width), bf),
            vmem((n, 8, 2, PAD, width), bf),
            vmem((n, PAD, width), bf),
            vmem((n, PAD, width), bf),
            sems(2 + n), sems(4),
            sems(n), sems(n),
            sems(n), sems(n, 8),
            sems(n), sems(n), sems(n), sems(n), sems(n), sems(n),
            sems(n), sems(n), sems(n), sems(n), sems(n), sems(n),
            sems(n), sems(n, 8),
            sems(n), sems(n),
        ],
        compiler_params=pltpu.CompilerParams(
            collective_id=0, has_side_effects=True, vmem_limit_bytes=62 * 1024 * 1024
        ),
        cost_estimate=pl.CostEstimate(
            flops=2 * 4 * lanes * model_width * units * 3,
            bytes_accessed=3 * model_width * units * 2,
            transcendentals=4 * lanes * units,
        ),
    )(tokens, expert_ids.T, gates.T, w_gate, w_up, w_down)


def solution(mesh):
    in_specs = (
        P(("expert", "dp"), None),
        P(("expert", "dp"), None),
        P(("expert", "dp"), None),
        P("expert", None, "dp"),
        P("expert", None, "dp"),
        P("expert", "dp", None),
    )
    out_specs = P(("expert", "dp"), None)
    return jax.shard_map(local, mesh=mesh, in_specs=in_specs, out_specs=out_specs, check_vma=False)
```

```python
import functools

import jax
import jax.numpy as jnp
from jax import lax
from jax.experimental import pallas as pl
from jax.experimental.pallas import tpu as pltpu
from jax.sharding import PartitionSpec as P

CAP = 2
PAD = 16
YS = 4
CHUNK = 1024
KINDS = "abababa"
ORDER_OUT = (
    14, 12, 10, 22, 8, 20, 18, 30, 9, 28, 38, 26, 16, 17, 36, 13, 46, 24, 34, 11, 25, 44, 32, 21, 42,
    54, 33, 40, 29, 19, 52, 41, 37, 62, 50, 27, 45, 48, 35, 57, 43, 60, 61, 65, 58, 68, 70, 56, 69, 59,
    66, 64, 67,
)
ORDER_BACK = (
    3, 4, 6, 1, 19, 12, 2, 5, 14, 0, 17, 21, 10, 27, 35, 25, 8, 20, 43, 33, 22, 29, 51, 18, 41, 37, 28,
    16, 30, 49, 45, 26, 36, 57, 38, 24, 34, 53, 32, 44, 46, 59, 42, 65, 40, 52, 54, 61, 50, 67, 48, 58,
    62, 69, 60, 56,
)
MESH = pl.DeviceIdType.MESH


def dot(a, b):
    return jnp.dot(a, b, preferred_element_type=jnp.float32)


def kernel(
    zs, ys, n, width,
    tok_ref, ids_ref, gates_ref, wg_hbm, wu_hbm, wd_hbm, out_ref,
    flip_i, flip_g, mtsend, mtbuf, mtopp, sel, zbuf, slot, rows, wg, wu, wd, acc_g, acc_u, hid,
    send_c, recv_c, send_x, recv_x, ret, retr, zsend, zrecv, last_s, last_r,
    w_sem, mt_sem, x_s, x_r, z_s, z_r, p_s, p_r, o_s, o_r, k_s, k_r,
    rc_s, rc_r, rx_s, rx_r, rp_s, rp_r, rz_s, rz_r, rl_s, rl_r,
):
    e = lax.axis_index("expert")
    q = lax.axis_index("dp")
    js = 2 * ys
    z, j = e // js, e % js
    y, xh = j // 2, j % 2
    xl, core = q // 2, q % 2
    topk, tok_rows = ids_ref.shape
    held = zs * CAP
    lanes = js * held
    kinds = [KINDS[c % len(KINDS)] for c in range(n)]

    planes = []
    for dy in range(ys):
        for dx in range(2):
            if dy or dx:
                there = ((y + dy) % ys) * 2 + (xh + dx) % 2
                side = xl if dx == 0 else 1 - xl
                planes.append(((z * js + there, side * 2 + core), there, side))
    columns = []
    for dz in range(1, zs):
        there = (z + dz) % zs
        columns.append(((there * js + j, q), there))
    long_hops, short_hops = zs // 2, zs - 1 - zs // 2
    step = 1 + core * (zs - 2)

    def at_z(hops, sign):
        return (z + zs * zs + sign * hops * step) % zs

    ahead, behind = (at_z(1, 1) * js + j, q), (at_z(1, -1) * js + j, q)
    mate = (e, xl * 2 + (1 - core))
    opp = (e, (1 - xl) * 2 + core)

    barrier = pltpu.get_barrier_semaphore()
    partners = [p[0] for p in planes] + [c[0] for c in columns] + [mate, opp]
    for partner in partners:
        pl.semaphore_signal(barrier, inc=1, device_id=partner, device_id_type=MESH)

    weights = [
        pltpu.make_async_copy(wg_hbm.at[0], wg, w_sem.at[0]),
        pltpu.make_async_copy(wu_hbm.at[0], wu, w_sem.at[1]),
    ] + [
        pltpu.make_async_copy(wd_hbm.at[0, :, pl.ds(c * width, width)], wd.at[c], w_sem.at[2 + c])
        for c in range(n)
    ]
    for copy in weights:
        copy.start()

    def remote(src, dst, send, recv, device):
        return pltpu.make_async_remote_copy(
            src_ref=src, dst_ref=dst, send_sem=send, recv_sem=recv,
            device_id=device, device_id_type=MESH,
        )

    for c in range(n):
        zbuf[c, z, 0] = jnp.zeros((PAD, width), jnp.bfloat16)
        zbuf[c, z, 0, 0:tok_rows, :] = tok_ref[:, c * width:(c + 1) * width]

    flip_i[...] = jnp.full(flip_i.shape, -1.0, jnp.float32)
    flip_i[0:topk, 0:tok_rows] = ids_ref[...].astype(jnp.float32)
    flip_g[...] = jnp.zeros(flip_g.shape, jnp.float32)
    flip_g[0:topk, 0:tok_rows] = gates_ref[...].astype(jnp.float32)
    ids = flip_i[...].T[0:PAD]
    gates = flip_g[...].T[0:PAD]
    lane = lax.broadcasted_iota(jnp.int32, (PAD, zs * lanes), 1)
    lane_expert = (lane // held).astype(jnp.float32)
    lane_slot = (lane % CAP).astype(jnp.float32)
    lower = (
        lax.broadcasted_iota(jnp.int32, (PAD, PAD), 0) > lax.broadcasted_iota(jnp.int32, (PAD, PAD), 1)
    ).astype(jnp.bfloat16)
    named = jnp.zeros(lane.shape, jnp.float32)
    weight = jnp.zeros(lane.shape, jnp.float32)
    for k in range(topk):
        match = ids[:, k:k + 1] == lane_expert
        named = named + jnp.where(match, 1.0, 0.0)
        weight = weight + jnp.where(match, gates[:, k:k + 1], 0.0)
    before = dot(lower, named.astype(jnp.bfloat16))
    mine = (before == lane_slot) & ((lane // CAP) % zs == z)
    routed = jnp.where(mine, weight, 0.0).astype(jnp.bfloat16)
    for plane in range(zs):
        mtsend[plane] = routed[:, plane * lanes:(plane + 1) * lanes]
    mtbuf[z] = mtsend[z]

    pl.semaphore_wait(barrier, len(partners))

    def sides(c):
        return 2 if kinds[c] == "b" else 1

    def swap_tokens(c):
        return remote(zbuf.at[c, z, 0], zbuf.at[c, z, 1], x_s.at[c], x_r.at[c], opp)

    def column_copy(c, origin, way, hop):
        part = zbuf.at[c, origin] if kinds[c] == "b" else zbuf.at[c, origin, 0]
        return remote(part, part, z_s.at[c], z_r.at[c, way * 4 + hop - 1], ahead if way == 0 else behind)

    def column_send(c, hop):
        if hop == 1:
            if kinds[c] == "b":
                swap_tokens(c).wait_recv()
            column_copy(c, z, 0, 1).start()
            column_copy(c, z, 1, 1).start()
            return
        if hop <= long_hops:
            column_copy(c, at_z(hop - 1, -1), 0, hop - 1).wait_recv()
            column_copy(c, at_z(hop - 1, -1), 0, hop).start()
        if hop <= short_hops:
            column_copy(c, at_z(hop - 1, 1), 1, hop - 1).wait_recv()
            column_copy(c, at_z(hop - 1, 1), 1, hop).start()

    def plane_send(c):
        column_copy(c, at_z(long_hops, -1), 0, long_hops).wait_recv()
        if short_hops:
            column_copy(c, at_z(short_hops, 1), 1, short_hops).wait_recv()
        for side in range(sides(c)):
            chosen = dot(sel[side], zbuf[c, :, side].reshape(zs * PAD, width)).astype(jnp.bfloat16)
            chosen = chosen.reshape(js, held, width)
            if kinds[c] == "a":
                slot[c, 0] = chosen
            else:
                for there in range(js):
                    slot[c, (xl + side + xh + there) % 2, there] = chosen[there]
        for device, there, dest in planes:
            for side in range(sides(c)):
                group = dest if kinds[c] == "a" else side
                src, dst = slot.at[c, side, there], rows.at[c, core, group, j]
                remote(src, dst, p_s.at[c], p_r.at[c], device).start()
        if kinds[c] == "a":
            rows[c, core, xl, j] = slot[c, 0, j]
        else:
            for side in range(2):
                rows[c, core, side, j] = slot[c, side, j]

    def plane_wait(buf, c, send, recv):
        part = buf.at[c, pl.ds(0, sides(c)), pl.ds(0, js - 1)]
        return remote(part, part, send.at[c], recv.at[c], mate)

    def to_opp(c):
        part = rows.at[c, core, xl]
        return remote(part, part, o_s.at[c], o_r.at[c], opp)

    def to_mate(c):
        part = rows.at[c, core]
        return remote(part, part, k_s.at[c], k_r.at[c], mate)

    def opp_send(c):
        plane_wait(slot, c, p_s, p_r).wait_recv()
        to_opp(c).start()

    def mate_send(c):
        if kinds[c] == "a":
            to_opp(c).wait_recv()
        else:
            plane_wait(slot, c, p_s, p_r).wait_recv()
        to_mate(c).start()

    multiplied = []

    def multiply(c):
        first = not multiplied
        multiplied.append(c)
        to_mate(c).wait_recv()
        if first:
            weights[0].wait()
            weights[1].wait()
        block = rows[c].reshape(4 * lanes, width)
        gate_part = dot(block, wg[c * width:(c + 1) * width, :])
        up_part = dot(block, wu[c * width:(c + 1) * width, :])
        acc_g[...] = gate_part if first else acc_g[...] + gate_part
        acc_u[...] = up_part if first else acc_u[...] + up_part

    def routes_out():
        for device, there in columns:
            remote(mtsend.at[there], mtbuf.at[z], mt_sem.at[0], mt_sem.at[1], device).start()

    def routes_wait():
        return remote(
            mtsend.at[pl.ds(0, zs - 1)], mtbuf.at[pl.ds(0, zs - 1)], mt_sem.at[0], mt_sem.at[1], mate
        )

    def routes_to_opp():
        return remote(mtbuf, mtopp, mt_sem.at[2], mt_sem.at[3], opp)

    def selection(buf):
        values = buf[...].reshape(zs * PAD, lanes).astype(jnp.float32)
        return jnp.where(values != 0.0, 1.0, 0.0).T.astype(jnp.bfloat16)

    def choose_own():
        routes_wait().wait_recv()
        routes_to_opp().start()
        sel[0] = selection(mtbuf)

    def choose_opp():
        routes_to_opp().wait_recv()
        sel[1] = selection(mtopp)

    both = [c for c in range(n) if kinds[c] == "b"]
    for c in both:
        swap_tokens(c).start()
    routes_out()
    hops = [functools.partial(column_send, hop=hop) for hop in range(1, 5)]
    steps = [None] + hops + [plane_send, opp_send, mate_send, multiply]
    chosen_own = chosen_opp = False
    for code in ORDER_OUT:
        number, c = code // 8, code % 8
        if not chosen_own and number >= 4:
            choose_own()
            chosen_own = True
        if not chosen_opp and number == 5 and kinds[c] == "b":
            choose_opp()
            chosen_opp = True
        steps[number](c)

    gate_out, up_out = acc_g[...], acc_u[...]
    hidden = gate_out / (1.0 + jnp.exp(-gate_out)) * up_out
    hid[...] = hidden.astype(jnp.bfloat16).reshape(hid.shape)
    for copy in weights[2:]:
        copy.wait()

    def sums_to_mate(c):
        return remote(send_c.at[c], recv_c.at[c], rc_s.at[c], rc_r.at[c], mate)

    def sums_to_opp(c):
        return remote(send_x.at[c], recv_x.at[c], rx_s.at[c], rx_r.at[c], opp)

    def core_sums(c):
        block = hid[1 - core].reshape(2 * lanes, hid.shape[-1])
        send_c[c] = dot(block, wd[c]).astype(jnp.bfloat16).reshape(2, lanes, width)
        sums_to_mate(c).start()

    def chip_sums(c):
        sums_to_mate(c).wait_recv()
        total = dot(hid[core, 1 - xl], wd[c]) + recv_c[c, 1 - xl].astype(jnp.float32)
        send_x[c] = total.astype(jnp.bfloat16)
        sums_to_opp(c).start()

    def plane_return(c):
        if kinds[c] == "a":
            sums_to_opp(c).wait_recv()
            total = (
                dot(hid[core, xl], wd[c])
                + recv_c[c, xl].astype(jnp.float32)
                + recv_x[c].astype(jnp.float32)
            )
            ret[c, 0] = total.astype(jnp.bfloat16).reshape(js, held, width)
        else:
            sums_to_mate(c).wait_recv()
            for side in range(2):
                total = dot(hid[core, side], wd[c]) + recv_c[c, side].astype(jnp.float32)
                ret[c, side] = total.astype(jnp.bfloat16).reshape(js, held, width)
        for device, there, _ in planes:
            for side in range(sides(c)):
                src, dst = ret.at[c, side, there], retr.at[c, side, j]
                remote(src, dst, rp_s.at[c], rp_r.at[c], device).start()
        for side in range(sides(c)):
            retr[c, side, j] = ret[c, side, j]

    def return_copy(c, target, way, hop):
        src, dst = zsend.at[c, target], zrecv.at[c, way * 4 + hop - 1]
        if kinds[c] == "a":
            src, dst = src.at[0], dst.at[0]
        return remote(
            src, dst,
            rz_s.at[c], rz_r.at[c, way * 4 + hop - 1], ahead if way == 0 else behind,
        )

    def token_sums(c):
        plane_wait(retr, c, rp_s, rp_r).wait_recv()
        for side in range(sides(c)):
            if kinds[c] == "a":
                block = retr[c, 0].reshape(lanes, width)
            else:
                block = jnp.concatenate(
                    [retr[c, (xl + side + xh + there) % 2, there] for there in range(js)], axis=0
                )
            mixing = (mtbuf if side == 0 else mtopp)[...].reshape(zs * PAD, lanes)
            zsend[c, :, side] = dot(mixing, block).astype(jnp.bfloat16).reshape(zs, PAD, width)
        return_copy(c, at_z(long_hops, 1), 0, 1).start()

    def add_in(c, target, way, hop):
        for side in range(sides(c)):
            total = zsend[c, target, side].astype(jnp.float32)
            total = total + zrecv[c, way * 4 + hop - 1, side].astype(jnp.float32)
            zsend[c, target, side] = total.astype(jnp.bfloat16)

    def return_send(c, hop):
        target = at_z(long_hops - hop + 1, 1)
        return_copy(c, target, 0, hop - 1).wait_recv()
        add_in(c, target, 0, hop - 1)
        return_copy(c, target, 0, hop).start()
        hop = hop - (long_hops - short_hops)
        if hop >= 1:
            target = at_z(short_hops - hop + 1, -1)
            if hop >= 2:
                return_copy(c, target, 1, hop - 1).wait_recv()
                add_in(c, target, 1, hop - 1)
            return_copy(c, target, 1, hop).start()

    def column_total(c, side):
        total = zsend[c, z, side].astype(jnp.float32)
        total = total + zrecv[c, long_hops - 1, side].astype(jnp.float32)
        if short_hops:
            total = total + zrecv[c, 4 + short_hops - 1, side].astype(jnp.float32)
        return total

    def swap_sums(c):
        return remote(last_s.at[c], last_r.at[c], rl_s.at[c], rl_r.at[c], opp)

    def columns_done(c):
        return_copy(c, z, 0, long_hops).wait_recv()
        if short_hops:
            return_copy(c, z, 1, short_hops).wait_recv()
        if kinds[c] == "b":
            last_s[c] = column_total(c, 1).astype(jnp.bfloat16)
            swap_sums(c).start()
        else:
            out_ref[:, c * width:(c + 1) * width] = column_total(c, 0).astype(jnp.bfloat16)[0:tok_rows]

    def finish(c):
        swap_sums(c).wait_recv()
        total = column_total(c, 0) + last_r[c].astype(jnp.float32)
        out_ref[:, c * width:(c + 1) * width] = total.astype(jnp.bfloat16)[0:tok_rows]

    hops = [functools.partial(return_send, hop=hop) for hop in range(2, 5)]
    steps = [core_sums, chip_sums, plane_return, token_sums] + hops + [columns_done, finish]
    for code in ORDER_BACK:
        steps[code // 8](code % 8)

    routes_wait().wait_send()
    routes_to_opp().wait_send()
    for c in range(n):
        if kinds[c] == "b":
            swap_tokens(c).wait_send()
            swap_sums(c).wait_send()
        else:
            to_opp(c).wait_send()
            sums_to_opp(c).wait_send()
        part = zbuf.at[c, pl.ds(0, zs - 1), pl.ds(0, sides(c))]
        remote(part, part, z_s.at[c], z_r.at[c, 0], mate).wait_send()
        plane_wait(slot, c, p_s, p_r).wait_send()
        to_mate(c).wait_send()
        sums_to_mate(c).wait_send()
        plane_wait(ret, c, rp_s, rp_r).wait_send()
        part = zsend.at[c, pl.ds(0, zs - 1), pl.ds(0, sides(c))]
        remote(part, part, rz_s.at[c], rz_r.at[c, 0], mate).wait_send()


def local(tokens, expert_ids, gates, w_gate, w_up, w_down):
    tok_rows, model_width = tokens.shape
    units = w_gate.shape[2]
    ys = YS
    js = 2 * ys
    zs = lax.axis_size("expert") // js
    width = min(CHUNK, model_width // 2)
    n = model_width // width
    held = zs * CAP
    lanes = js * held
    bf = jnp.bfloat16
    vmem = pltpu.VMEM
    sems = lambda *shape: pltpu.SemaphoreType.DMA(shape)
    return pl.pallas_call(
        functools.partial(kernel, zs, ys, n, width),
        out_shape=jax.ShapeDtypeStruct((tok_rows, model_width), bf),
        in_specs=[pl.BlockSpec(memory_space=pltpu.VMEM)] * 3 + [pl.BlockSpec(memory_space=pl.ANY)] * 3,
        out_specs=pl.BlockSpec(memory_space=pltpu.VMEM),
        scratch_shapes=[
            vmem((128, 128), jnp.float32),
            vmem((128, 128), jnp.float32),
            vmem((zs, PAD, lanes), bf),
            vmem((zs, PAD, lanes), bf),
            vmem((zs, PAD, lanes), bf),
            vmem((2, lanes, zs * PAD), bf),
            vmem((n, zs, 2, PAD, width), bf),
            vmem((n, 2, js, held, width), bf),
            vmem((n, 2, 2, js, held, width), bf),
            vmem((model_width, units), bf),
            vmem((model_width, units), bf),
            vmem((n, units, width), bf),
            vmem((4 * lanes, units), jnp.float32),
            vmem((4 * lanes, units), jnp.float32),
            vmem((2, 2, lanes, units), bf),
            vmem((n, 2, lanes, width), bf),
            vmem((n, 2, lanes, width), bf),
            vmem((n, lanes, width), bf),
            vmem((n, lanes, width), bf),
            vmem((n, 2, js, held, width), bf),
            vmem((n, 2, js, held, width), bf),
            vmem((n, zs, 2, PAD, width), bf),
            vmem((n, 8, 2, PAD, width), bf),
            vmem((n, PAD, width), bf),
            vmem((n, PAD, width), bf),
            sems(2 + n), sems(4),
            sems(n), sems(n),
            sems(n), sems(n, 8),
            sems(n), sems(n), sems(n), sems(n), sems(n), sems(n),
            sems(n), sems(n), sems(n), sems(n), sems(n), sems(n),
            sems(n), sems(n, 8),
            sems(n), sems(n),
        ],
        compiler_params=pltpu.CompilerParams(
            collective_id=0, has_side_effects=True, vmem_limit_bytes=62 * 1024 * 1024
        ),
        cost_estimate=pl.CostEstimate(
            flops=2 * 4 * lanes * model_width * units * 3,
            bytes_accessed=3 * model_width * units * 2,
            transcendentals=4 * lanes * units,
        ),
    )(tokens, expert_ids.T, gates.T, w_gate, w_up, w_down)


def solution(mesh):
    in_specs = (
        P(("expert", "dp"), None),
        P(("expert", "dp"), None),
        P(("expert", "dp"), None),
        P("expert", None, "dp"),
        P("expert", None, "dp"),
        P("expert", "dp", None),
    )
    out_specs = P(("expert", "dp"), None)
    return jax.shard_map(local, mesh=mesh, in_specs=in_specs, out_specs=out_specs, check_vma=False)
```

```python
import functools

import jax
import jax.numpy as jnp
from jax import lax
from jax.experimental import pallas as pl
from jax.experimental.pallas import tpu as pltpu
from jax.sharding import PartitionSpec as P

CAP = 2
PAD = 16
YS = 4
CHUNK = 1024
KINDS = "abababa"
ORDER_OUT = (
    14, 12, 10, 22, 8, 20, 18, 30, 9, 28, 38, 26, 16, 17, 36, 13, 46, 24, 34, 11, 25, 44, 32, 21, 42,
    54, 33, 40, 29, 19, 52, 41, 37, 62, 50, 27, 45, 48, 35, 57, 43, 60, 61, 65, 58, 68, 70, 56, 69, 59,
    66, 64, 67,
)
ORDER_BACK = (
    3, 4, 6, 1, 19, 12, 2, 5, 14, 0, 17, 21, 10, 27, 35, 25, 8, 20, 43, 33, 22, 29, 51, 18, 41, 37, 28,
    16, 30, 49, 45, 26, 36, 57, 38, 24, 34, 53, 32, 44, 46, 59, 42, 65, 40, 52, 54, 61, 50, 67, 48, 58,
    62, 69, 60, 56,
)
MESH = pl.DeviceIdType.MESH


def dot(a, b):
    return jnp.dot(a, b, preferred_element_type=jnp.float32)


def kernel(
    zs, ys, n, width,
    tok_ref, ids_ref, gates_ref, wg_hbm, wu_hbm, wd_hbm, out_ref,
    flip_i, flip_g, mtsend, mtbuf, mtopp, sel, zbuf, slot, rows, wg, wu, wd, acc_g, acc_u, hid,
    send_c, recv_c, send_x, recv_x, ret, retr, zsend, zrecv, last_s, last_r,
    w_sem, mt_sem, x_s, x_r, z_s, z_r, p_s, p_r, o_s, o_r, k_s, k_r,
    rc_s, rc_r, rx_s, rx_r, rp_s, rp_r, rz_s, rz_r, rl_s, rl_r,
):
    e = lax.axis_index("expert")
    q = lax.axis_index("dp")
    js = 2 * ys
    z, j = e // js, e % js
    y, xh = j // 2, j % 2
    xl, core = q // 2, q % 2
    topk, tok_rows = ids_ref.shape
    held = zs * CAP
    lanes = js * held
    kinds = [KINDS[c % len(KINDS)] for c in range(n)]

    planes = []
    for dy in range(ys):
        for dx in range(2):
            if dy or dx:
                there = ((y + dy) % ys) * 2 + (xh + dx) % 2
                side = xl if dx == 0 else 1 - xl
                planes.append(((z * js + there, side * 2 + core), there, side))
    columns = []
    for dz in range(1, zs):
        there = (z + dz) % zs
        columns.append(((there * js + j, q), there))
    long_hops, short_hops = zs // 2, zs - 1 - zs // 2
    step = 1 + core * (zs - 2)

    def at_z(hops, sign):
        return (z + zs * zs + sign * hops * step) % zs

    ahead, behind = (at_z(1, 1) * js + j, q), (at_z(1, -1) * js + j, q)
    mate = (e, xl * 2 + (1 - core))
    opp = (e, (1 - xl) * 2 + core)

    barrier = pltpu.get_barrier_semaphore()
    partners = [p[0] for p in planes] + [c[0] for c in columns] + [mate, opp]
    for partner in partners:
        pl.semaphore_signal(barrier, inc=1, device_id=partner, device_id_type=MESH)

    weights = [
        pltpu.make_async_copy(wg_hbm.at[0], wg, w_sem.at[0]),
        pltpu.make_async_copy(wu_hbm.at[0], wu, w_sem.at[1]),
    ] + [
        pltpu.make_async_copy(wd_hbm.at[0, :, pl.ds(c * width, width)], wd.at[c], w_sem.at[2 + c])
        for c in range(n)
    ]
    for copy in weights:
        copy.start()

    def remote(src, dst, send, recv, device):
        return pltpu.make_async_remote_copy(
            src_ref=src, dst_ref=dst, send_sem=send, recv_sem=recv,
            device_id=device, device_id_type=MESH,
        )

    for c in range(n):
        zbuf[c, z, 0] = jnp.zeros((PAD, width), jnp.bfloat16)
        zbuf[c, z, 0, 0:tok_rows, :] = tok_ref[:, c * width:(c + 1) * width]

    pl.semaphore_wait(barrier, len(partners))

    def sides(c):
        return 2 if kinds[c] == "b" else 1

    def swap_tokens(c):
        return remote(zbuf.at[c, z, 0], zbuf.at[c, z, 1], x_s.at[c], x_r.at[c], opp)

    def column_copy(c, origin, way, hop):
        part = zbuf.at[c, origin] if kinds[c] == "b" else zbuf.at[c, origin, 0]
        return remote(part, part, z_s.at[c], z_r.at[c, way * 4 + hop - 1], ahead if way == 0 else behind)

    def column_send(c, hop):
        if hop == 1:
            if kinds[c] == "b":
                swap_tokens(c).wait_recv()
            column_copy(c, z, 0, 1).start()
            column_copy(c, z, 1, 1).start()
            return
        if hop <= long_hops:
            column_copy(c, at_z(hop - 1, -1), 0, hop - 1).wait_recv()
            column_copy(c, at_z(hop - 1, -1), 0, hop).start()
        if hop <= short_hops:
            column_copy(c, at_z(hop - 1, 1), 1, hop - 1).wait_recv()
            column_copy(c, at_z(hop - 1, 1), 1, hop).start()

    def plane_send(c):
        column_copy(c, at_z(long_hops, -1), 0, long_hops).wait_recv()
        if short_hops:
            column_copy(c, at_z(short_hops, 1), 1, short_hops).wait_recv()
        for side in range(sides(c)):
            chosen = dot(sel[side], zbuf[c, :, side].reshape(zs * PAD, width)).astype(jnp.bfloat16)
            chosen = chosen.reshape(js, held, width)
            if kinds[c] == "a":
                slot[c, 0] = chosen
            else:
                for there in range(js):
                    slot[c, (xl + side + xh + there) % 2, there] = chosen[there]
        for device, there, dest in planes:
            for side in range(sides(c)):
                group = dest if kinds[c] == "a" else side
                src, dst = slot.at[c, side, there], rows.at[c, core, group, j]
                remote(src, dst, p_s.at[c], p_r.at[c], device).start()
        if kinds[c] == "a":
            rows[c, core, xl, j] = slot[c, 0, j]
        else:
            for side in range(2):
                rows[c, core, side, j] = slot[c, side, j]

    def plane_wait(buf, c, send, recv):
        part = buf.at[c, pl.ds(0, sides(c)), pl.ds(0, js - 1)]
        return remote(part, part, send.at[c], recv.at[c], mate)

    def to_opp(c):
        part = rows.at[c, core, xl]
        return remote(part, part, o_s.at[c], o_r.at[c], opp)

    def to_mate(c):
        part = rows.at[c, core]
        return remote(part, part, k_s.at[c], k_r.at[c], mate)

    def opp_send(c):
        plane_wait(slot, c, p_s, p_r).wait_recv()
        to_opp(c).start()

    def mate_send(c):
        if kinds[c] == "a":
            to_opp(c).wait_recv()
        else:
            plane_wait(slot, c, p_s, p_r).wait_recv()
        to_mate(c).start()

    multiplied = []

    def multiply(c):
        first = not multiplied
        multiplied.append(c)
        to_mate(c).wait_recv()
        if first:
            weights[0].wait()
            weights[1].wait()
        block = rows[c].reshape(4 * lanes, width)
        gate_part = dot(block, wg[c * width:(c + 1) * width, :])
        up_part = dot(block, wu[c * width:(c + 1) * width, :])
        acc_g[...] = gate_part if first else acc_g[...] + gate_part
        acc_u[...] = up_part if first else acc_u[...] + up_part

    def make_routes():
        flip_i[...] = jnp.full(flip_i.shape, -1.0, jnp.float32)
        flip_i[0:topk, 0:tok_rows] = ids_ref[...].astype(jnp.float32)
        flip_g[...] = jnp.zeros(flip_g.shape, jnp.float32)
        flip_g[0:topk, 0:tok_rows] = gates_ref[...].astype(jnp.float32)
        ids = flip_i[...].T[0:PAD]
        gates = flip_g[...].T[0:PAD]
        lane = lax.broadcasted_iota(jnp.int32, (PAD, zs * lanes), 1)
        lane_expert = (lane // held).astype(jnp.float32)
        lane_slot = (lane % CAP).astype(jnp.float32)
        lower = (
            lax.broadcasted_iota(jnp.int32, (PAD, PAD), 0) > lax.broadcasted_iota(jnp.int32, (PAD, PAD), 1)
        ).astype(jnp.bfloat16)
        named = jnp.zeros(lane.shape, jnp.float32)
        weight = jnp.zeros(lane.shape, jnp.float32)
        for k in range(topk):
            match = ids[:, k:k + 1] == lane_expert
            named = named + jnp.where(match, 1.0, 0.0)
            weight = weight + jnp.where(match, gates[:, k:k + 1], 0.0)
        before = dot(lower, named.astype(jnp.bfloat16))
        mine = (before == lane_slot) & ((lane // CAP) % zs == z)
        routed = jnp.where(mine, weight, 0.0).astype(jnp.bfloat16)
        for plane in range(zs):
            mtsend[plane] = routed[:, plane * lanes:(plane + 1) * lanes]
        mtbuf[z] = mtsend[z]

    def routes_out():
        for device, there in columns:
            remote(mtsend.at[there], mtbuf.at[z], mt_sem.at[0], mt_sem.at[1], device).start()

    def routes_wait():
        return remote(
            mtsend.at[pl.ds(0, zs - 1)], mtbuf.at[pl.ds(0, zs - 1)], mt_sem.at[0], mt_sem.at[1], mate
        )

    def routes_to_opp():
        return remote(mtbuf, mtopp, mt_sem.at[2], mt_sem.at[3], opp)

    def selection(buf):
        values = buf[...].reshape(zs * PAD, lanes).astype(jnp.float32)
        return jnp.where(values != 0.0, 1.0, 0.0).T.astype(jnp.bfloat16)

    def choose_own():
        routes_wait().wait_recv()
        routes_to_opp().start()
        sel[0] = selection(mtbuf)

    def choose_opp():
        routes_to_opp().wait_recv()
        sel[1] = selection(mtopp)

    both = [c for c in range(n) if kinds[c] == "b"]
    for c in both:
        swap_tokens(c).start()
    hops = [functools.partial(column_send, hop=hop) for hop in range(1, 5)]
    steps = [None] + hops + [plane_send, opp_send, mate_send, multiply]
    chosen_own = chosen_opp = False
    for place, code in enumerate(ORDER_OUT):
        number, c = code // 8, code % 8
        if place == 1:
            make_routes()
            routes_out()
        if not chosen_own and number >= 4:
            choose_own()
            chosen_own = True
        if not chosen_opp and number == 5 and kinds[c] == "b":
            choose_opp()
            chosen_opp = True
        steps[number](c)

    gate_out, up_out = acc_g[...], acc_u[...]
    hidden = gate_out / (1.0 + jnp.exp(-gate_out)) * up_out
    hid[...] = hidden.astype(jnp.bfloat16).reshape(hid.shape)
    for copy in weights[2:]:
        copy.wait()

    def sums_to_mate(c):
        return remote(send_c.at[c], recv_c.at[c], rc_s.at[c], rc_r.at[c], mate)

    def sums_to_opp(c):
        return remote(send_x.at[c], recv_x.at[c], rx_s.at[c], rx_r.at[c], opp)

    def core_sums(c):
        block = hid[1 - core].reshape(2 * lanes, hid.shape[-1])
        send_c[c] = dot(block, wd[c]).astype(jnp.bfloat16).reshape(2, lanes, width)
        sums_to_mate(c).start()

    def chip_sums(c):
        sums_to_mate(c).wait_recv()
        total = dot(hid[core, 1 - xl], wd[c]) + recv_c[c, 1 - xl].astype(jnp.float32)
        send_x[c] = total.astype(jnp.bfloat16)
        sums_to_opp(c).start()

    def plane_return(c):
        if kinds[c] == "a":
            sums_to_opp(c).wait_recv()
            total = (
                dot(hid[core, xl], wd[c])
                + recv_c[c, xl].astype(jnp.float32)
                + recv_x[c].astype(jnp.float32)
            )
            ret[c, 0] = total.astype(jnp.bfloat16).reshape(js, held, width)
        else:
            sums_to_mate(c).wait_recv()
            for side in range(2):
                total = dot(hid[core, side], wd[c]) + recv_c[c, side].astype(jnp.float32)
                ret[c, side] = total.astype(jnp.bfloat16).reshape(js, held, width)
        for device, there, _ in planes:
            for side in range(sides(c)):
                src, dst = ret.at[c, side, there], retr.at[c, side, j]
                remote(src, dst, rp_s.at[c], rp_r.at[c], device).start()
        for side in range(sides(c)):
            retr[c, side, j] = ret[c, side, j]

    def return_copy(c, target, way, hop):
        src, dst = zsend.at[c, target], zrecv.at[c, way * 4 + hop - 1]
        if kinds[c] == "a":
            src, dst = src.at[0], dst.at[0]
        return remote(
            src, dst,
            rz_s.at[c], rz_r.at[c, way * 4 + hop - 1], ahead if way == 0 else behind,
        )

    def token_sums(c):
        plane_wait(retr, c, rp_s, rp_r).wait_recv()
        for side in range(sides(c)):
            if kinds[c] == "a":
                block = retr[c, 0].reshape(lanes, width)
            else:
                block = jnp.concatenate(
                    [retr[c, (xl + side + xh + there) % 2, there] for there in range(js)], axis=0
                )
            mixing = (mtbuf if side == 0 else mtopp)[...].reshape(zs * PAD, lanes)
            zsend[c, :, side] = dot(mixing, block).astype(jnp.bfloat16).reshape(zs, PAD, width)
        return_copy(c, at_z(long_hops, 1), 0, 1).start()

    def add_in(c, target, way, hop):
        for side in range(sides(c)):
            total = zsend[c, target, side].astype(jnp.float32)
            total = total + zrecv[c, way * 4 + hop - 1, side].astype(jnp.float32)
            zsend[c, target, side] = total.astype(jnp.bfloat16)

    def return_send(c, hop):
        target = at_z(long_hops - hop + 1, 1)
        return_copy(c, target, 0, hop - 1).wait_recv()
        add_in(c, target, 0, hop - 1)
        return_copy(c, target, 0, hop).start()
        hop = hop - (long_hops - short_hops)
        if hop >= 1:
            target = at_z(short_hops - hop + 1, -1)
            if hop >= 2:
                return_copy(c, target, 1, hop - 1).wait_recv()
                add_in(c, target, 1, hop - 1)
            return_copy(c, target, 1, hop).start()

    def column_total(c, side):
        total = zsend[c, z, side].astype(jnp.float32)
        total = total + zrecv[c, long_hops - 1, side].astype(jnp.float32)
        if short_hops:
            total = total + zrecv[c, 4 + short_hops - 1, side].astype(jnp.float32)
        return total

    def swap_sums(c):
        return remote(last_s.at[c], last_r.at[c], rl_s.at[c], rl_r.at[c], opp)

    def columns_done(c):
        return_copy(c, z, 0, long_hops).wait_recv()
        if short_hops:
            return_copy(c, z, 1, short_hops).wait_recv()
        if kinds[c] == "b":
            last_s[c] = column_total(c, 1).astype(jnp.bfloat16)
            swap_sums(c).start()
        else:
            out_ref[:, c * width:(c + 1) * width] = column_total(c, 0).astype(jnp.bfloat16)[0:tok_rows]

    def finish(c):
        swap_sums(c).wait_recv()
        total = column_total(c, 0) + last_r[c].astype(jnp.float32)
        out_ref[:, c * width:(c + 1) * width] = total.astype(jnp.bfloat16)[0:tok_rows]

    hops = [functools.partial(return_send, hop=hop) for hop in range(2, 5)]
    steps = [core_sums, chip_sums, plane_return, token_sums] + hops + [columns_done, finish]
    for code in ORDER_BACK:
        steps[code // 8](code % 8)

    routes_wait().wait_send()
    routes_to_opp().wait_send()
    for c in range(n):
        if kinds[c] == "b":
            swap_tokens(c).wait_send()
            swap_sums(c).wait_send()
        else:
            to_opp(c).wait_send()
            sums_to_opp(c).wait_send()
        part = zbuf.at[c, pl.ds(0, zs - 1), pl.ds(0, sides(c))]
        remote(part, part, z_s.at[c], z_r.at[c, 0], mate).wait_send()
        plane_wait(slot, c, p_s, p_r).wait_send()
        to_mate(c).wait_send()
        sums_to_mate(c).wait_send()
        plane_wait(ret, c, rp_s, rp_r).wait_send()
        part = zsend.at[c, pl.ds(0, zs - 1), pl.ds(0, sides(c))]
        remote(part, part, rz_s.at[c], rz_r.at[c, 0], mate).wait_send()


def local(tokens, expert_ids, gates, w_gate, w_up, w_down):
    tok_rows, model_width = tokens.shape
    units = w_gate.shape[2]
    ys = YS
    js = 2 * ys
    zs = lax.axis_size("expert") // js
    width = min(CHUNK, model_width // 2)
    n = model_width // width
    held = zs * CAP
    lanes = js * held
    bf = jnp.bfloat16
    vmem = pltpu.VMEM
    sems = lambda *shape: pltpu.SemaphoreType.DMA(shape)
    return pl.pallas_call(
        functools.partial(kernel, zs, ys, n, width),
        out_shape=jax.ShapeDtypeStruct((tok_rows, model_width), bf),
        in_specs=[pl.BlockSpec(memory_space=pltpu.VMEM)] * 3 + [pl.BlockSpec(memory_space=pl.ANY)] * 3,
        out_specs=pl.BlockSpec(memory_space=pltpu.VMEM),
        scratch_shapes=[
            vmem((128, 128), jnp.float32),
            vmem((128, 128), jnp.float32),
            vmem((zs, PAD, lanes), bf),
            vmem((zs, PAD, lanes), bf),
            vmem((zs, PAD, lanes), bf),
            vmem((2, lanes, zs * PAD), bf),
            vmem((n, zs, 2, PAD, width), bf),
            vmem((n, 2, js, held, width), bf),
            vmem((n, 2, 2, js, held, width), bf),
            vmem((model_width, units), bf),
            vmem((model_width, units), bf),
            vmem((n, units, width), bf),
            vmem((4 * lanes, units), jnp.float32),
            vmem((4 * lanes, units), jnp.float32),
            vmem((2, 2, lanes, units), bf),
            vmem((n, 2, lanes, width), bf),
            vmem((n, 2, lanes, width), bf),
            vmem((n, lanes, width), bf),
            vmem((n, lanes, width), bf),
            vmem((n, 2, js, held, width), bf),
            vmem((n, 2, js, held, width), bf),
            vmem((n, zs, 2, PAD, width), bf),
            vmem((n, 8, 2, PAD, width), bf),
            vmem((n, PAD, width), bf),
            vmem((n, PAD, width), bf),
            sems(2 + n), sems(4),
            sems(n), sems(n),
            sems(n), sems(n, 8),
            sems(n), sems(n), sems(n), sems(n), sems(n), sems(n),
            sems(n), sems(n), sems(n), sems(n), sems(n), sems(n),
            sems(n), sems(n, 8),
            sems(n), sems(n),
        ],
        compiler_params=pltpu.CompilerParams(
            collective_id=0, has_side_effects=True, vmem_limit_bytes=62 * 1024 * 1024
        ),
        cost_estimate=pl.CostEstimate(
            flops=2 * 4 * lanes * model_width * units * 3,
            bytes_accessed=3 * model_width * units * 2,
            transcendentals=4 * lanes * units,
        ),
    )(tokens, expert_ids.T, gates.T, w_gate, w_up, w_down)


def solution(mesh):
    in_specs = (
        P(("expert", "dp"), None),
        P(("expert", "dp"), None),
        P(("expert", "dp"), None),
        P("expert", None, "dp"),
        P("expert", None, "dp"),
        P("expert", "dp", None),
    )
    out_specs = P(("expert", "dp"), None)
    return jax.shard_map(local, mesh=mesh, in_specs=in_specs, out_specs=out_specs, check_vma=False)
```
